256 devices in a mesh: pairs: 128 (over z, x, y_lo, core), emb: 2 (over y_hi).
Axes of the slice: x: 4, y: 4 (y_hi: 2, y_lo: 2; y = y_hi * 2 + y_lo), z: 8, core: 2. Of those that a mesh axis runs over, the one named last changes fastest.
Arguments:
- round_bits: int32 [2], replicated, may hold values from 0 to 6
- image_embed: bfloat16 [65536, 1152], P('pairs', 'emb'), may hold values from -0.46289062 to 0.46289062
- text_embed: bfloat16 [65536, 1152], P('pairs', 'emb'), may hold values from -0.46289062 to 0.46289062
Outputs:
- image_grad: float32 [65536, 1152], P('pairs', 'emb')
- text_grad: float32 [65536, 1152], P('pairs', 'emb')
The draws below stay inside these ranges and needn't reach their ends.
All inputs are finite; a program needn't handle non-finite values.
Results may differ from the reference program's by a relative error of at most 0.0025.
Values may be sent and summed in bfloat16 or wider, within the bound.
A program may use at most 64 MiB of HBM per device.

```python
import jax
import jax.numpy as jnp
from jax import lax

D = 1152
TOK_DEV = 512
ROUNDS = 2
TOKENS = 65536
PAIR_BITS = 7
N_PAIRS = 128


def shard_levels(key, extent, cuts, least, largest):
    gain = 1.0
    for position, shards_of in cuts:
        heights = jax.random.uniform(jax.random.fold_in(jax.random.fold_in(key, 6), position), (shards_of,), jnp.float32, least / len(cuts), largest / len(cuts))
        gain = gain * jnp.repeat(jnp.exp(heights), extent[position] // shards_of).reshape((-1,) + (1,) * (len(extent) - 1 - position))
    return gain


def bell_draw(stream_key, dims, scale, bound, cuts=(), held_as=jnp.bfloat16):
    array = scale * jax.random.normal(stream_key, dims, jnp.float32)
    if cuts:
        array = array * shard_levels(stream_key, dims, cuts, -0.22, 0.18)
    return jnp.clip(array, -bound, bound).astype(held_as)


def setup_inputs(seed: int = 0) -> dict:
    seeds = jax.random.split(jax.random.key(seed), 4)
    return {
        "round_bits": jax.random.randint(seeds[0], (ROUNDS,), 0, PAIR_BITS).astype(jnp.int32),
        "image_embed": bell_draw(seeds[1], (TOKENS, D), (0.45 * D ** -0.25), 0.46289062, ((0, 128), (1, 2))),
        "text_embed": bell_draw(seeds[2], (TOKENS, D), (0.45 * D ** -0.25), 0.46289062, ((0, 128), (1, 2))),
    }


logit_scale = 10.0
logit_bias = -1.0


def pair_weights(scores, labels):
    logits = logit_scale * scores + logit_bias
    return (-labels * logit_scale * jax.nn.sigmoid(-labels * logits)).astype(jnp.bfloat16)


def contract_last(left, right):
    return lax.dot_general(left, right, (((1,), (1,)), ((), ())), preferred_element_type=jnp.float32)


def contract_first(left, right):
    return lax.dot_general(left, right, (((0,), (0,)), ((), ())), preferred_element_type=jnp.float32)


def reference(round_bits, image_embed, text_embed):
    diagonal_mask = jnp.eye(TOK_DEV, dtype=jnp.float32)
    own_labels = 2.0 * diagonal_mask - 1.0

    def one_block(block_index):
        start_row = (block_index * TOK_DEV).astype(jnp.int32)
        image_own = lax.dynamic_slice_in_dim(image_embed, start_row, TOK_DEV, 0)
        text_own = lax.dynamic_slice_in_dim(text_embed, start_row, TOK_DEV, 0)
        own_weights = pair_weights(contract_last(image_own, text_own), own_labels)
        image_grad = jnp.dot(own_weights, text_own, preferred_element_type=jnp.float32)
        text_grad = contract_first(own_weights, image_own)
        for round_index in range(ROUNDS):
            flip = jnp.left_shift(jnp.int32(1), round_bits[round_index].astype(jnp.int32)).astype(jnp.int32)
            partner = jnp.bitwise_xor(block_index, flip).astype(jnp.int32)
            start_partner = (partner * TOK_DEV).astype(jnp.int32)
            image_other = lax.dynamic_slice_in_dim(image_embed, start_partner, TOK_DEV, 0)
            text_other = lax.dynamic_slice_in_dim(text_embed, start_partner, TOK_DEV, 0)
            row_weights = pair_weights(contract_last(image_own, text_other), -1.0)
            image_grad = image_grad + jnp.dot(row_weights, text_other, preferred_element_type=jnp.float32)
            column_weights = pair_weights(contract_last(image_other, text_own), -1.0)
            text_grad = text_grad + contract_first(column_weights, image_other)
        return image_grad, text_grad

    image_grad, text_grad = lax.map(one_block, jnp.arange(N_PAIRS, dtype=jnp.int32))
    return image_grad.reshape(TOKENS, D), text_grad.reshape(TOKENS, D)
```

```python
import functools

import jax
import jax.numpy as jnp
from jax import lax
from jax.experimental import pallas as pl
from jax.experimental.pallas import tpu as pltpu
from jax.sharding import PartitionSpec as P

logit_scale = 10.0
logit_bias = -1.0
PAIR_BITS = 7
CHUNKS = 4
LEAD = 2
MESH = pl.DeviceIdType.MESH


def flipped(index, bit):
    return index + (1 - 2 * ((index // bit) % 2)) * bit


def last(left, right):
    return lax.dot_general(
        left, right, (((1,), (1,)), ((), ())), preferred_element_type=jnp.float32
    )


def first(left, right):
    return lax.dot_general(
        left, right, (((0,), (0,)), ((), ())), preferred_element_type=jnp.float32
    )


def kernel(
    bits,
    image_hbm,
    text_hbm,
    image_out,
    text_out,
    image,
    texts,
    partial,
    partial_out,
    partial_in,
    weights,
    extra_out,
    extra_in,
    image_sum,
    text_sum,
    local_sem,
    text_send,
    text_recv,
    part_send,
    part_recv,
    extra_send,
    extra_recv,
    out_sem,
):
    rows = image.shape[0]
    n = rows // CHUNKS
    rounds = len(bits)
    items = (rounds + 1) * CHUNKS
    pair = lax.axis_index("pairs")
    half = lax.axis_index("emb")

    def partner(r):
        if rounds == 1:
            return flipped(pair, bits[0])
        met = [flipped(pair, bit) for bit in bits]
        return met[0] + (met[1] - met[0]) * r

    def tile_rows(t, c):
        return pl.ds(pl.multiple_of(t * rows + c * n, n), n)

    def text_copy(r, c):
        return pltpu.make_async_remote_copy(
            src_ref=text_hbm.at[pl.ds(pl.multiple_of(c * n, n), n)],
            dst_ref=texts.at[tile_rows(r + 1, c)],
            send_sem=text_send.at[r, c],
            recv_sem=text_recv.at[r, c],
            device_id=(partner(r), half),
            device_id_type=MESH,
        )

    def part_copy(t, c):
        return pltpu.make_async_remote_copy(
            src_ref=partial_out.at[tile_rows(t, c)],
            dst_ref=partial_in.at[tile_rows(t, c)],
            send_sem=part_send.at[t, c],
            recv_sem=part_recv.at[t, c],
            device_id=(pair, 1 - half),
            device_id_type=MESH,
        )

    def extra_copy(r, c):
        return pltpu.make_async_remote_copy(
            src_ref=extra_out.at[tile_rows(r, c)],
            dst_ref=extra_in.at[tile_rows(r, c)],
            send_sem=extra_send.at[r, c],
            recv_sem=extra_recv.at[r, c],
            device_id=(partner(r), half),
            device_id_type=MESH,
        )

    def text_out_copy(c):
        chunk = pl.ds(pl.multiple_of(c * n, n), n)
        return pltpu.make_async_copy(
            text_sum.at[chunk], text_out.at[chunk], out_sem.at[c]
        )

    def item(i):
        inner = i - LEAD
        met = (inner >= 0) & (inner < rounds * CHUNKS)
        tile = jnp.where(met, 1 + inner % rounds, 0)
        chunk = jnp.where(
            met, inner // rounds, jnp.where(inner < 0, i, i - rounds * CHUNKS)
        )
        return tile, chunk

    own_image = pltpu.make_async_copy(image_hbm, image, local_sem.at[0])
    own_text = pltpu.make_async_copy(text_hbm, texts.at[pl.ds(0, rows)], local_sem.at[1])
    own_image.start()
    own_text.start()
    barrier = pltpu.get_barrier_semaphore()
    pl.semaphore_signal(barrier, inc=1, device_id=(pair, 1 - half), device_id_type=MESH)
    for r in range(rounds):
        pl.semaphore_signal(
            barrier, inc=1, device_id=(partner(r), half), device_id_type=MESH
        )
    pl.semaphore_wait(barrier, rounds + 1)
    for c in range(CHUNKS):
        for r in range(rounds):
            text_copy(r, c).start()
    own_image.wait()
    own_text.wait()

    @pl.loop(0, items)
    def _(i):
        t, c = item(i)

        @pl.when(t > 0)
        def _():
            text_copy(t - 1, c).wait_recv()

        where = tile_rows(t, c)
        scores = last(texts[where, :], image[...])
        partial[where, :] = scores
        partial_out[where, :] = scores.astype(jnp.bfloat16)
        part_copy(t, c).start()

    @pl.loop(0, items)
    def _(i):
        t, c = item(i)
        part_copy(t, c).wait_recv()
        where = tile_rows(t, c)
        scores = partial[where, :] + partial_in[where, :].astype(jnp.float32)
        logits = logit_scale * scores + logit_bias
        text_row = c * n + lax.broadcasted_iota(jnp.int32, scores.shape, 0)
        image_row = lax.broadcasted_iota(jnp.int32, scores.shape, 1)
        same = text_row == image_row + t * (2 * rows)
        labels = jnp.where(same, 1.0, -1.0)
        chunk = -labels * logit_scale * jax.nn.sigmoid(-labels * logits)
        chunk = chunk.astype(jnp.bfloat16)
        if rounds == 1:
            chunk = jnp.where(t > 0, chunk * 2, chunk)
        weights[where, :] = chunk
        grad = jnp.dot(chunk, image[...], preferred_element_type=jnp.float32)

        @pl.when(t == 0)
        def _():
            text_sum[pl.ds(pl.multiple_of(c * n, n), n), :] = grad

        @pl.when(t > 0)
        def _():
            extra_out[tile_rows(t - 1, c), :] = grad.astype(jnp.bfloat16)
            extra_copy(t - 1, c).start()

    @pl.loop(0, rows // 128)
    def _(m):
        block = pl.ds(pl.multiple_of(m * 128, 128), 128)
        image_sum[block, :] = first(weights[:, block], texts[...])

    image_copy = pltpu.make_async_copy(image_sum, image_out, local_sem.at[0])
    image_copy.start()

    @pl.loop(0, CHUNKS)
    def _(c):
        chunk = pl.ds(pl.multiple_of(c * n, n), n)
        for r in range(rounds):
            extra_copy(r, c).wait_recv()
            text_sum[chunk, :] += extra_in[tile_rows(r, c), :].astype(jnp.float32)
        text_out_copy(c).start()

    @pl.loop(0, CHUNKS)
    def _(c):
        for r in range(rounds):
            text_copy(r, c).wait_send()
            extra_copy(r, c).wait_send()
        for t in range(rounds + 1):
            part_copy(t, c).wait_send()
        text_out_copy(c).wait()

    image_copy.wait()


def meet(bits, collective_id, image, text):
    rows, width = image.shape
    rounds = len(bits)
    tiles = rounds + 1
    out = jax.ShapeDtypeStruct((rows, width), jnp.float32)
    return pl.pallas_call(
        functools.partial(kernel, bits),
        out_shape=(out, out),
        in_specs=[pl.BlockSpec(memory_space=pl.ANY)] * 2,
        out_specs=(pl.BlockSpec(memory_space=pl.ANY),) * 2,
        scratch_shapes=[
            pltpu.VMEM((rows, width), jnp.bfloat16),
            pltpu.VMEM((tiles * rows, width), jnp.bfloat16),
            pltpu.VMEM((tiles * rows, rows), jnp.float32),
            pltpu.VMEM((tiles * rows, rows), jnp.bfloat16),
            pltpu.VMEM((tiles * rows, rows), jnp.bfloat16),
            pltpu.VMEM((tiles * rows, rows), jnp.bfloat16),
            pltpu.VMEM((rounds * rows, width), jnp.bfloat16),
            pltpu.VMEM((rounds * rows, width), jnp.bfloat16),
            pltpu.VMEM((rows, width), jnp.float32),
            pltpu.VMEM((rows, width), jnp.float32),
            pltpu.SemaphoreType.DMA((2,)),
            pltpu.SemaphoreType.DMA((rounds, CHUNKS)),
            pltpu.SemaphoreType.DMA((rounds, CHUNKS)),
            pltpu.SemaphoreType.DMA((tiles, CHUNKS)),
            pltpu.SemaphoreType.DMA((tiles, CHUNKS)),
            pltpu.SemaphoreType.DMA((rounds, CHUNKS)),
            pltpu.SemaphoreType.DMA((rounds, CHUNKS)),
            pltpu.SemaphoreType.DMA((CHUNKS,)),
        ],
        compiler_params=pltpu.CompilerParams(
            collective_id=collective_id,
            has_side_effects=True,
            vmem_limit_bytes=40 << 20,
        ),
        cost_estimate=pl.CostEstimate(
            flops=2 * (3 * tiles) * rows * rows * width,
            bytes_accessed=12 * rows * width,
            transcendentals=tiles * rows * rows,
        ),
    )(image, text)


def shards(round_bits, image_embed, text_embed):
    low = jnp.minimum(round_bits[0], round_bits[1])
    high = jnp.maximum(round_bits[0], round_bits[1])
    branches = []
    for a in range(PAIR_BITS):
        for b in range(a, PAIR_BITS):
            bits = (1 << a,) if a == b else (1 << a, 1 << b)
            branches.append(functools.partial(meet, bits, len(branches) + 1))
    which = low * PAIR_BITS - low * (low - 1) // 2 + (high - low)
    return lax.switch(which, branches, image_embed, text_embed)


def solution(mesh):
    placed = (P(), P("pairs", "emb"), P("pairs", "emb"))
    return jax.shard_map(
        shards,
        mesh=mesh,
        in_specs=placed,
        out_specs=(P("pairs", "emb"), P("pairs", "emb")),
        check_vma=False,
    )
```

```python
import functools

import jax
import jax.numpy as jnp
from jax import lax
from jax.experimental import pallas as pl
from jax.experimental.pallas import tpu as pltpu
from jax.sharding import PartitionSpec as P

logit_scale = 10.0
logit_bias = -1.0
PAIR_BITS = 7
CHUNKS = 4
LEAD = 2
MESH = pl.DeviceIdType.MESH


def flipped(index, bit):
    return index + (1 - 2 * ((index // bit) % 2)) * bit


def last(left, right):
    return lax.dot_general(
        left, right, (((1,), (1,)), ((), ())), preferred_element_type=jnp.float32
    )


def first(left, right):
    return lax.dot_general(
        left, right, (((0,), (0,)), ((), ())), preferred_element_type=jnp.float32
    )


def kernel(
    bits,
    image_hbm,
    text_hbm,
    image_out,
    text_out,
    image,
    texts,
    partial,
    partial_out,
    partial_in,
    weights,
    extra_out,
    extra_in,
    image_sum,
    text_sum,
    local_sem,
    text_send,
    text_recv,
    part_send,
    part_recv,
    extra_send,
    extra_recv,
    out_sem,
):
    rows = image.shape[1]
    n = rows // CHUNKS
    rounds = len(bits)
    items = (rounds + 1) * CHUNKS
    pair = lax.axis_index("pairs")
    half = lax.axis_index("emb")

    def partner(r):
        if rounds == 1:
            return flipped(pair, bits[0])
        met = [flipped(pair, bit) for bit in bits]
        return met[0] + (met[1] - met[0]) * r

    def place(t, c):
        return pl.ds(pl.multiple_of(t * rows + c * n, n), n)

    def text_copy(r, c):
        return pltpu.make_async_remote_copy(
            src_ref=text_hbm.at[:, place(0, c)],
            dst_ref=texts.at[:, place(r + 1, c)],
            send_sem=text_send.at[r, c],
            recv_sem=text_recv.at[r, c],
            device_id=(partner(r), half),
            device_id_type=MESH,
        )

    def part_copy(t, c):
        return pltpu.make_async_remote_copy(
            src_ref=partial_out.at[place(t, c)],
            dst_ref=partial_in.at[place(t, c)],
            send_sem=part_send.at[t, c],
            recv_sem=part_recv.at[t, c],
            device_id=(pair, 1 - half),
            device_id_type=MESH,
        )

    def extra_copy(r, c):
        return pltpu.make_async_remote_copy(
            src_ref=extra_out.at[:, place(r, c)],
            dst_ref=extra_in.at[:, place(r, c)],
            send_sem=extra_send.at[r, c],
            recv_sem=extra_recv.at[r, c],
            device_id=(partner(r), half),
            device_id_type=MESH,
        )

    def text_out_copy(c):
        return pltpu.make_async_copy(
            text_sum.at[:, place(0, c)], text_out.at[:, place(0, c)], out_sem.at[c]
        )

    def item(i):
        inner = i - LEAD
        met = (inner >= 0) & (inner < rounds * CHUNKS)
        tile = jnp.where(met, 1 + inner % rounds, 0)
        chunk = jnp.where(
            met, inner // rounds, jnp.where(inner < 0, i, i - rounds * CHUNKS)
        )
        return tile, chunk

    own_image = pltpu.make_async_copy(image_hbm, image, local_sem.at[0])
    own_text = pltpu.make_async_copy(text_hbm, texts.at[:, pl.ds(0, rows)], local_sem.at[1])
    own_image.start()
    own_text.start()
    barrier = pltpu.get_barrier_semaphore()
    pl.semaphore_signal(barrier, inc=1, device_id=(pair, 1 - half), device_id_type=MESH)
    for r in range(rounds):
        pl.semaphore_signal(
            barrier, inc=1, device_id=(partner(r), half), device_id_type=MESH
        )
    pl.semaphore_wait(barrier, rounds + 1)
    for c in range(CHUNKS):
        for r in range(rounds):
            text_copy(r, c).start()
    own_image.wait()
    own_text.wait()

    @pl.loop(0, items)
    def _(i):
        t, c = item(i)

        @pl.when(t > 0)
        def _():
            text_copy(t - 1, c).wait_recv()

        where = place(t, c)
        scores = first(texts[:, where], image[...])
        partial[where, :] = scores
        partial_out[where, :] = scores.astype(jnp.bfloat16)
        part_copy(t, c).start()

    @pl.loop(0, items)
    def _(i):
        t, c = item(i)
        part_copy(t, c).wait_recv()
        where = place(t, c)
        scores = partial[where, :] + partial_in[where, :].astype(jnp.float32)
        logits = logit_scale * scores + logit_bias
        text_row = c * n + lax.broadcasted_iota(jnp.int32, scores.shape, 0)
        image_row = lax.broadcasted_iota(jnp.int32, scores.shape, 1)
        same = text_row == image_row + t * (2 * rows)
        labels = jnp.where(same, 1.0, -1.0)
        chunk = -labels * logit_scale * jax.nn.sigmoid(-labels * logits)
        chunk = chunk.astype(jnp.bfloat16)
        if rounds == 1:
            chunk = jnp.where(t > 0, chunk * 2, chunk)
        weights[where, :] = chunk
        grad = last(image[...], chunk)

        @pl.when(t == 0)
        def _():
            text_sum[:, place(0, c)] = grad

        @pl.when(t > 0)
        def _():
            extra_out[:, place(t - 1, c)] = grad.astype(jnp.bfloat16)
            extra_copy(t - 1, c).start()

    @pl.loop(0, rows // 256)
    def _(m):
        block = pl.ds(pl.multiple_of(m * 256, 256), 256)
        image_sum[:, block] = jnp.dot(
            texts[...], weights[:, block], preferred_element_type=jnp.float32
        )

    image_copy = pltpu.make_async_copy(image_sum, image_out, local_sem.at[0])
    image_copy.start()

    @pl.loop(0, CHUNKS)
    def _(c):
        for r in range(rounds):
            extra_copy(r, c).wait_recv()
            text_sum[:, place(0, c)] += extra_in[:, place(r, c)].astype(jnp.float32)
        text_out_copy(c).start()

    @pl.loop(0, CHUNKS)
    def _(c):
        for r in range(rounds):
            text_copy(r, c).wait_send()
            extra_copy(r, c).wait_send()
        for t in range(rounds + 1):
            part_copy(t, c).wait_send()
        text_out_copy(c).wait()

    image_copy.wait()


def meet(bits, collective_id, image, text):
    width, rows = image.shape
    rounds = len(bits)
    tiles = rounds + 1
    out = jax.ShapeDtypeStruct((width, rows), jnp.float32)
    return pl.pallas_call(
        functools.partial(kernel, bits),
        out_shape=(out, out),
        in_specs=[pl.BlockSpec(memory_space=pl.ANY)] * 2,
        out_specs=(pl.BlockSpec(memory_space=pl.ANY),) * 2,
        scratch_shapes=[
            pltpu.VMEM((width, rows), jnp.bfloat16),
            pltpu.VMEM((width, tiles * rows), jnp.bfloat16),
            pltpu.VMEM((tiles * rows, rows), jnp.float32),
            pltpu.VMEM((tiles * rows, rows), jnp.bfloat16),
            pltpu.VMEM((tiles * rows, rows), jnp.bfloat16),
            pltpu.VMEM((tiles * rows, rows), jnp.bfloat16),
            pltpu.VMEM((width, rounds * rows), jnp.bfloat16),
            pltpu.VMEM((width, rounds * rows), jnp.bfloat16),
            pltpu.VMEM((width, rows), jnp.float32),
            pltpu.VMEM((width, rows), jnp.float32),
            pltpu.SemaphoreType.DMA((2,)),
            pltpu.SemaphoreType.DMA((rounds, CHUNKS)),
            pltpu.SemaphoreType.DMA((rounds, CHUNKS)),
            pltpu.SemaphoreType.DMA((tiles, CHUNKS)),
            pltpu.SemaphoreType.DMA((tiles, CHUNKS)),
            pltpu.SemaphoreType.DMA((rounds, CHUNKS)),
            pltpu.SemaphoreType.DMA((rounds, CHUNKS)),
            pltpu.SemaphoreType.DMA((CHUNKS,)),
        ],
        compiler_params=pltpu.CompilerParams(
            collective_id=collective_id,
            has_side_effects=True,
            vmem_limit_bytes=40 << 20,
        ),
        cost_estimate=pl.CostEstimate(
            flops=2 * (3 * tiles) * rows * rows * width,
            bytes_accessed=12 * rows * width,
            transcendentals=tiles * rows * rows,
        ),
    )(image, text)


def shards(round_bits, image_embed, text_embed):
    low = jnp.minimum(round_bits[0], round_bits[1])
    high = jnp.maximum(round_bits[0], round_bits[1])
    branches = []
    for a in range(PAIR_BITS):
        for b in range(a, PAIR_BITS):
            bits = (1 << a,) if a == b else (1 << a, 1 << b)
            branches.append(functools.partial(meet, bits, len(branches) + 1))
    which = low * PAIR_BITS - low * (low - 1) // 2 + (high - low)
    image_grad, text_grad = lax.switch(which, branches, image_embed.T, text_embed.T)
    return image_grad.T, text_grad.T


def solution(mesh):
    placed = (P(), P("pairs", "emb"), P("pairs", "emb"))
    return jax.shard_map(
        shards,
        mesh=mesh,
        in_specs=placed,
        out_specs=(P("pairs", "emb"), P("pairs", "emb")),
        check_vma=False,
    )
```

```python
import functools

import jax
import jax.numpy as jnp
from jax import lax
from jax.experimental import pallas as pl
from jax.experimental.pallas import tpu as pltpu
from jax.sharding import PartitionSpec as P

logit_scale = 10.0
logit_bias = -1.0
PAIR_BITS = 7
CHUNKS = 4
LEAD = 2
CHAINED = ((4, 8), (16, 64), (32, 64))
MESH = pl.DeviceIdType.MESH


def flipped(index, bit):
    return index + (1 - 2 * ((index // bit) % 2)) * bit


def last(left, right):
    return lax.dot_general(
        left, right, (((1,), (1,)), ((), ())), preferred_element_type=jnp.float32
    )


def first(left, right):
    return lax.dot_general(
        left, right, (((0,), (0,)), ((), ())), preferred_element_type=jnp.float32
    )


class Plan:
    def __init__(self, bits):
        self.bits = bits
        self.chain = bits in CHAINED
        self.rounds = len(bits)
        self.tiles = 1 + self.rounds
        lead = CHUNKS if self.chain else LEAD
        head = ([0], 0, lead)
        tail = ([0], lead, CHUNKS - lead)
        met = [(list(range(1, self.tiles)), 0, CHUNKS)]
        self.score_order = [head, *met, tail]
        if self.chain:
            met = [([2], 0, CHUNKS), ([1], 0, CHUNKS)]
        self.weight_order = [head, *met, tail]
        self.early = self.tiles * CHUNKS - (CHUNKS - lead)


def placed_at(order, i):
    start = 0
    tile, chunk = 0, 0
    for tiles, low, count in order:
        if not count:
            continue
        inner = i - start
        here = tiles[0]
        for k in range(1, len(tiles)):
            here = jnp.where(inner % len(tiles) == k, tiles[k], here)
        tile = jnp.where(inner >= 0, here, tile)
        chunk = jnp.where(inner >= 0, low + inner // len(tiles), chunk)
        start += count * len(tiles)
    return tile, chunk


def kernel(
    plan,
    image_hbm,
    text_hbm,
    image_out,
    text_out,
    held,
    partial,
    partial_out,
    partial_in,
    weights,
    extra_out,
    extra_in,
    image_sum,
    text_sum,
    local_sem,
    held_send,
    held_recv,
    part_send,
    part_recv,
    extra_send,
    extra_recv,
    out_sem,
):
    rows = image_sum.shape[1]
    n = rows // CHUNKS
    tall = image_sum.shape[0] // 2
    tiles = plan.tiles
    items = tiles * CHUNKS
    pair = lax.axis_index("pairs")
    half = lax.axis_index("emb")
    met = [flipped(pair, bit) for bit in plan.bits]
    across = flipped(met[0], plan.bits[1]) if plan.chain else None

    def place(t, c):
        return pl.ds(pl.multiple_of(t * rows + c * n, n), n)

    def back_to(t):
        if plan.rounds == 1:
            return met[0]
        return met[0] + ((across if plan.chain else met[1]) - met[0]) * (t - 1)

    def remote(src, dst, sends, recvs, t, c, device):
        return pltpu.make_async_remote_copy(
            src_ref=src,
            dst_ref=dst,
            send_sem=sends.at[t, c],
            recv_sem=recvs.at[t, c],
            device_id=device,
            device_id_type=MESH,
        )

    def held_copy(t, c, source=text_hbm, slot=0):
        return remote(
            source.at[:, place(slot, c)],
            held.at[:, place(t, c)],
            held_send,
            held_recv,
            t,
            c,
            (back_to(t), half),
        )

    def part_copy(t, c):
        return remote(
            partial_out.at[place(t, c)],
            partial_in.at[place(t, c)],
            part_send,
            part_recv,
            t,
            c,
            (pair, 1 - half),
        )

    def extra_copy(t, c):
        return remote(
            extra_out.at[:, place(t - 1, c)],
            extra_in.at[:, place(t - 1, c)],
            extra_send,
            extra_recv,
            t,
            c,
            (back_to(t), half),
        )

    def text_out_copy(c):
        return pltpu.make_async_copy(
            text_sum.at[:, place(0, c)], text_out.at[:, place(0, c)], out_sem.at[c]
        )

    own_text = pltpu.make_async_copy(text_hbm, held.at[:, pl.ds(0, rows)], local_sem.at[0])
    own_image = pltpu.make_async_copy(
        image_hbm, held.at[:, pl.ds(tiles * rows, rows)], local_sem.at[1]
    )
    own_text.start()
    own_image.start()

    peers = [(pair, 1 - half)] + [(block, half) for block in met]
    if plan.chain:
        peers.append((across, half))
    barrier = pltpu.get_barrier_semaphore()
    for peer in peers:
        pl.semaphore_signal(barrier, inc=1, device_id=peer, device_id_type=MESH)
    pl.semaphore_wait(barrier, len(peers))

    adds = plan.rounds - plan.chain

    @pl.loop(0, adds * CHUNKS)
    def _(i):
        held_copy(1 + i % adds, i // adds).start()

    own_text.wait()
    own_image.wait()

    @pl.loop(0, items)
    def _(i):
        t, c = placed_at(plan.score_order, i)

        @pl.when(t > 0)
        def _():
            held_copy(t, c).wait_recv()

        if plan.chain:

            @pl.when(t == 1)
            def _():
                held_copy(2, c, held, 1).start()

        where = place(t, c)
        scores = first(held[:, where], held[:, pl.ds(tiles * rows, rows)])
        partial[where, :] = scores
        partial_out[where, :] = scores.astype(jnp.bfloat16)
        part_copy(t, c).start()

    def weigh(i):
        t, c = placed_at(plan.weight_order, i)
        part_copy(t, c).wait_recv()
        where = place(t, c)
        scores = partial[where, :] + partial_in[where, :].astype(jnp.float32)
        logits = logit_scale * scores + logit_bias
        text_row = c * n + lax.broadcasted_iota(jnp.int32, scores.shape, 0)
        image_row = lax.broadcasted_iota(jnp.int32, scores.shape, 1)
        same = text_row == image_row + t * (2 * rows)
        labels = jnp.where(same, 1.0, -1.0)
        chunk = -labels * logit_scale * jax.nn.sigmoid(-labels * logits)
        if plan.rounds == 1:
            chunk = chunk * jnp.where(t > 0, 2.0, 1.0)
        chunk = chunk.astype(jnp.bfloat16)
        weights[where, :] = chunk
        if plan.chain:

            @pl.when(t == 1)
            def _():
                extra_copy(2, c).wait_recv()

        @pl.loop(0, 2)
        def _(m):
            down = pl.ds(pl.multiple_of(m * tall, tall), tall)
            grad = last(held[down, pl.ds(tiles * rows, rows)], weights[where, :])

            @pl.when(t == 0)
            def _():
                text_sum[down, place(0, c)] = grad

            @pl.when(t > 0)
            def _():
                extra_out[down, place(t - 1, c)] = grad.astype(jnp.bfloat16)

            if plan.chain:

                @pl.when(t == 1)
                def _():
                    extra_out[down, place(0, c)] = (
                        grad + extra_in[down, place(1, c)].astype(jnp.float32)
                    ).astype(jnp.bfloat16)

        @pl.when(t > 0)
        def _():
            extra_copy(t, c).start()

    def add_image(i):
        blocks = 4
        low = jnp.where(i == items, 0, blocks)
        high = jnp.where(i == items, blocks, blocks * tiles)
        if plan.early == items:
            low = 0
            high = jnp.where(i == items, blocks * tiles, 0)

        @pl.loop(low, high)
        def _(m):
            t = m // blocks
            depth = pl.ds(pl.multiple_of(t * rows, rows), rows)
            down = pl.ds(pl.multiple_of(m // 2 % 2 * tall, tall), tall)
            block = pl.ds(pl.multiple_of(m % 2 * 256, 256), 256)
            product = jnp.dot(
                held[down, depth], weights[depth, block], preferred_element_type=jnp.float32
            )
            begins = t == (0 if plan.early == items else 1)
            image_sum[down, block] = product + jnp.where(
                begins, 0.0, image_sum[down, block]
            )

    @pl.loop(0, items + 1)
    def _(i):
        @pl.when((i == plan.early) | (i == items))
        def _():
            add_image(i)

        @pl.when(i < items)
        def _():
            weigh(i)

    image_copy = pltpu.make_async_copy(image_sum, image_out, local_sem.at[0])
    image_copy.start()

    @pl.loop(0, adds * CHUNKS)
    def _(i):
        t, c = 1 + i % adds, i // adds
        extra_copy(t, c).wait_recv()
        text_sum[:, place(0, c)] += extra_in[:, place(t - 1, c)].astype(jnp.float32)

        @pl.when(t == adds)
        def _():
            text_out_copy(c).start()

    @pl.loop(0, items)
    def _(i):
        t, c = i // CHUNKS, i % CHUNKS
        part_copy(t, c).wait_send()

        @pl.when(t > 0)
        def _():
            held_copy(t, c).wait_send()
            extra_copy(t, c).wait_send()

        @pl.when(t == 0)
        def _():
            text_out_copy(c).wait()

    image_copy.wait()


def meet(bits, collective_id, image, text):
    plan = Plan(bits)
    width, rows = image.shape
    tiles = plan.tiles
    out = jax.ShapeDtypeStruct((width, rows), jnp.float32)
    pairs_of = pltpu.SemaphoreType.DMA((tiles, CHUNKS))
    return pl.pallas_call(
        functools.partial(kernel, plan),
        out_shape=(out, out),
        in_specs=[pl.BlockSpec(memory_space=pl.ANY)] * 2,
        out_specs=(pl.BlockSpec(memory_space=pl.ANY),) * 2,
        scratch_shapes=[
            pltpu.VMEM((width, (tiles + 1) * rows), jnp.bfloat16),
            pltpu.VMEM((tiles * rows, rows), jnp.float32),
            pltpu.VMEM((tiles * rows, rows), jnp.bfloat16),
            pltpu.VMEM((tiles * rows, rows), jnp.bfloat16),
            pltpu.VMEM((tiles * rows, rows), jnp.bfloat16),
            pltpu.VMEM((width, plan.rounds * rows), jnp.bfloat16),
            pltpu.VMEM((width, plan.rounds * rows), jnp.bfloat16),
            pltpu.VMEM((width, rows), jnp.float32),
            pltpu.VMEM((width, rows), jnp.float32),
            pltpu.SemaphoreType.DMA((2,)),
            *[pairs_of] * 6,
            pltpu.SemaphoreType.DMA((CHUNKS,)),
        ],
        compiler_params=pltpu.CompilerParams(
            collective_id=collective_id,
            has_side_effects=True,
            vmem_limit_bytes=40 << 20,
        ),
        cost_estimate=pl.CostEstimate(
            flops=2 * (3 * tiles) * rows * rows * width,
            bytes_accessed=12 * rows * width,
            transcendentals=tiles * rows * rows,
        ),
    )(image, text)


def pick(round_bits, which):
    low = jnp.minimum(round_bits[0], round_bits[1])
    high = jnp.maximum(round_bits[0], round_bits[1])
    which[0] = high + 6 * low - ((low * (low - 1)) >> 1)


def deliver(image_from, text_from, image_out, text_out, sem):
    copies = [
        pltpu.make_async_copy(image_from, image_out, sem.at[0]),
        pltpu.make_async_copy(text_from, text_out, sem.at[1]),
    ]
    for copy in copies:
        copy.start()
    for copy in copies:
        copy.wait()


def shards(round_bits, image_embed, text_embed):
    branches = []
    for a in range(PAIR_BITS):
        for b in range(a, PAIR_BITS):
            bits = (1 << a,) if a == b else (1 << a, 1 << b)
            branches.append(functools.partial(meet, bits, len(branches) + 1))
    which = pl.pallas_call(
        pick,
        out_shape=jax.ShapeDtypeStruct((1,), jnp.int32),
        in_specs=[pl.BlockSpec(memory_space=pltpu.SMEM)],
        out_specs=pl.BlockSpec(memory_space=pltpu.SMEM),
    )(round_bits)
    grads = lax.switch(which[0], branches, image_embed.T, text_embed.T)
    image_grad, text_grad = pl.pallas_call(
        deliver,
        out_shape=tuple(jax.ShapeDtypeStruct(g.shape, g.dtype) for g in grads),
        in_specs=[pl.BlockSpec(memory_space=pl.ANY)] * 2,
        out_specs=(pl.BlockSpec(memory_space=pl.ANY),) * 2,
        scratch_shapes=[pltpu.SemaphoreType.DMA((2,))],
    )(*grads)
    return image_grad.T, text_grad.T


def solution(mesh):
    placed = (P(), P("pairs", "emb"), P("pairs", "emb"))
    return jax.shard_map(
        shards,
        mesh=mesh,
        in_specs=placed,
        out_specs=(P("pairs", "emb"), P("pairs", "emb")),
        check_vma=False,
    )
```

```python
import functools

import jax
import jax.numpy as jnp
from jax import lax
from jax.experimental import pallas as pl
from jax.experimental.pallas import tpu as pltpu
from jax.sharding import PartitionSpec as P

logit_scale = 10.0
logit_bias = -1.0
PAIR_BITS = 7
CHUNKS = 4
CHAINED = ((4, 8), (16, 64), (32, 64))
MESH = pl.DeviceIdType.MESH


def flipped(index, bit):
    return index + (1 - 2 * ((index // bit) % 2)) * bit


def last(left, right):
    return lax.dot_general(
        left, right, (((1,), (1,)), ((), ())), preferred_element_type=jnp.float32
    )


def first(left, right):
    return lax.dot_general(
        left, right, (((0,), (0,)), ((), ())), preferred_element_type=jnp.float32
    )


SCORE, WEIGH, IMAGE, ADD = range(4)


def a(tile, chunk):
    return SCORE, tile, chunk


def b(tile, chunk):
    return WEIGH, tile, chunk


def i(low, high):
    return IMAGE, low, high


def d(tile, chunk):
    return ADD, tile, chunk


ONE = [
    a(0, 0), a(0, 1), a(1, 0), a(1, 1), b(0, 0), b(0, 1), b(1, 0), a(1, 2),
    b(1, 1), a(1, 3), a(0, 2), a(0, 3), b(1, 2), b(1, 3), i(1, 1), b(0, 2),
    d(1, 0), d(1, 1), d(1, 2), b(0, 3), i(0, 0), d(1, 3),
]
TWO = [
    a(0, 0), a(0, 1), a(1, 0), a(2, 0), a(1, 1), a(2, 1), b(0, 0), b(0, 1),
    b(1, 0), b(2, 0), a(1, 2), a(2, 2), b(1, 1), b(2, 1), a(1, 3), a(2, 3),
    a(0, 2), a(0, 3), b(1, 2), b(2, 2), b(1, 3), b(2, 3), i(1, 2), b(0, 2),
    d(1, 0), d(2, 0), d(1, 1), d(2, 1), d(1, 2), d(2, 2), b(0, 3), i(0, 0),
    d(1, 3), d(2, 3),
]
CHAIN = [
    a(0, 0), a(0, 1), a(0, 2), a(0, 3), a(1, 0), b(0, 0), a(1, 1), b(0, 1),
    a(2, 0), b(0, 2), a(1, 2), b(0, 3), a(2, 1), b(2, 0), a(1, 3), a(2, 2),
    b(2, 1), a(2, 3), b(2, 2), b(1, 0), b(2, 3), b(1, 1), b(1, 2), b(1, 3),
    i(0, 2), d(1, 0), d(1, 1), d(1, 2), d(1, 3),
]


class Plan:
    def __init__(self, bits):
        self.bits = bits
        self.rounds = len(bits)
        self.tiles = 1 + self.rounds
        self.chain = bits in CHAINED
        self.steps = CHAIN if self.chain else TWO if self.rounds == 2 else ONE
        images = [step for step in self.steps if step[0] == IMAGE]
        self.image_first = images[0][1]


def step_at(order, i):
    codes = [16 * kind + 4 * tile + chunk for kind, tile, chunk in order]
    word = 0
    for k in range(0, len(codes), 5):
        packed = sum(code << (6 * m) for m, code in enumerate(codes[k : k + 5]))
        word = jnp.where(i // 5 == k // 5, packed, word)
    code = lax.shift_right_logical(word, 6 * (i % 5)) % 64
    return code // 16, code // 4 % 4, code % 4


def kernel(
    plan,
    image_hbm,
    text_hbm,
    image_sum,
    text_sum,
    held,
    partial,
    partial_out,
    partial_in,
    weights,
    extra_out,
    extra_in,
    local_sem,
    held_send,
    held_recv,
    part_send,
    part_recv,
    extra_send,
    extra_recv,
):
    rows = image_sum.shape[1]
    n = rows // CHUNKS
    tall = image_sum.shape[0] // 2
    tiles = plan.tiles
    own = pl.ds(tiles * rows, rows)
    items = tiles * CHUNKS
    pair = lax.axis_index("pairs")
    half = lax.axis_index("emb")
    met = [flipped(pair, bit) for bit in plan.bits]
    across = flipped(met[0], plan.bits[1]) if plan.chain else None

    def place(t, c):
        return pl.ds(pl.multiple_of(t * rows + c * n, n), n)

    def back_to(t):
        if plan.rounds == 1:
            return met[0]
        return met[0] + ((across if plan.chain else met[1]) - met[0]) * (t - 1)

    def remote(src, dst, sends, recvs, t, c, device):
        return pltpu.make_async_remote_copy(
            src_ref=src,
            dst_ref=dst,
            send_sem=sends.at[t, c],
            recv_sem=recvs.at[t, c],
            device_id=device,
            device_id_type=MESH,
        )

    def held_copy(t, c, source=text_hbm, slot=0):
        return remote(
            source.at[:, place(slot, c)],
            held.at[:, place(t, c)],
            held_send,
            held_recv,
            t,
            c,
            (back_to(t), half),
        )

    def part_copy(t, c):
        return remote(
            partial_out.at[place(t, c)],
            partial_in.at[place(t, c)],
            part_send,
            part_recv,
            t,
            c,
            (pair, 1 - half),
        )

    def extra_copy(t, c):
        return remote(
            extra_out.at[:, place(t - 1, c)],
            extra_in.at[:, place(t - 1, c)],
            extra_send,
            extra_recv,
            t,
            c,
            (back_to(t), half),
        )

    own_text = pltpu.make_async_copy(text_hbm, held.at[:, pl.ds(0, rows)], local_sem.at[0])
    own_image = pltpu.make_async_copy(
        image_hbm, held.at[:, pl.ds(tiles * rows, rows)], local_sem.at[1]
    )
    own_text.start()
    own_image.start()

    peers = [(pair, 1 - half)] + [(block, half) for block in met]
    if plan.chain:
        peers.append((across, half))
    barrier = pltpu.get_barrier_semaphore()
    for peer in peers:
        pl.semaphore_signal(barrier, inc=1, device_id=peer, device_id_type=MESH)
    pl.semaphore_wait(barrier, len(peers))

    adds = plan.rounds - plan.chain

    @pl.loop(0, adds * CHUNKS)
    def _(i):
        held_copy(1 + i % adds, i // adds).start()

    own_text.wait()
    own_image.wait()

    def score(t, c):
        @pl.when(t > 0)
        def _():
            held_copy(t, c).wait_recv()

        if plan.chain:

            @pl.when(t == 1)
            def _():
                held_copy(2, c, held, 1).start()

        where = place(t, c)
        scores = first(held[:, where], held[:, own])
        partial[where, :] = scores
        partial_out[where, :] = scores.astype(jnp.bfloat16)
        part_copy(t, c).start()

    def weigh(t, c):
        part_copy(t, c).wait_recv()
        where = place(t, c)
        scores = partial[where, :] + partial_in[where, :].astype(jnp.float32)
        logits = logit_scale * scores + logit_bias
        text_row = c * n + lax.broadcasted_iota(jnp.int32, scores.shape, 0)
        image_row = lax.broadcasted_iota(jnp.int32, scores.shape, 1)
        same = text_row == image_row + t * (2 * rows)
        labels = jnp.where(same, 1.0, -1.0)
        chunk = -labels * logit_scale * jax.nn.sigmoid(-labels * logits)
        if plan.rounds == 1:
            chunk = chunk * jnp.where(t > 0, 2.0, 1.0)
        chunk = chunk.astype(jnp.bfloat16)
        weights[where, :] = chunk
        if plan.chain:

            @pl.when(t == 1)
            def _():
                extra_copy(2, c).wait_recv()

        @pl.loop(0, 2)
        def _(m):
            down = pl.ds(pl.multiple_of(m * tall, tall), tall)
            grad = last(held[down, own], weights[where, :])

            @pl.when(t == 0)
            def _():
                text_sum[down, place(0, c)] = grad

            @pl.when(t > 0)
            def _():
                extra_out[down, place(t - 1, c)] = grad.astype(jnp.bfloat16)

            if plan.chain:

                @pl.when(t == 1)
                def _():
                    extra_out[down, place(0, c)] = (
                        grad + extra_in[down, place(1, c)].astype(jnp.float32)
                    ).astype(jnp.bfloat16)

        @pl.when(t > 0)
        def _():
            extra_copy(t, c).start()

    def add_image(low, high):
        @pl.loop(low * 4, high * 4 + 4)
        def _(m):
            t = m // 4
            depth = pl.ds(pl.multiple_of(t * rows, rows), rows)
            down = pl.ds(pl.multiple_of(m // 2 % 2 * tall, tall), tall)
            block = pl.ds(pl.multiple_of(m % 2 * 256, 256), 256)
            product = jnp.dot(
                held[down, depth], weights[depth, block], preferred_element_type=jnp.float32
            )
            image_sum[down, block] = product + jnp.where(
                t == plan.image_first, 0.0, image_sum[down, block]
            )

    @pl.loop(0, len(plan.steps))
    def _(i):
        kind, t, c = step_at(plan.steps, i)

        @pl.when(kind == SCORE)
        def _():
            score(t, c)

        @pl.when(kind == WEIGH)
        def _():
            weigh(t, c)

        @pl.when(kind == IMAGE)
        def _():
            add_image(t, c)

        @pl.when(kind == ADD)
        def _():
            extra_copy(t, c).wait_recv()
            text_sum[:, place(0, c)] += extra_in[:, place(t - 1, c)].astype(jnp.float32)

    @pl.loop(0, items)
    def _(i):
        t, c = i // CHUNKS, i % CHUNKS
        part_copy(t, c).wait_send()

        @pl.when(t > 0)
        def _():
            held_copy(t, c).wait_send()
            extra_copy(t, c).wait_send()


def meet(bits, collective_id, image, text):
    plan = Plan(bits)
    width, rows = image.shape
    tiles = plan.tiles
    out = jax.ShapeDtypeStruct((width, rows), jnp.float32)
    pairs_of = pltpu.SemaphoreType.DMA((tiles, CHUNKS))
    return pl.pallas_call(
        functools.partial(kernel, plan),
        out_shape=(out, out),
        in_specs=[pl.BlockSpec(memory_space=pl.ANY)] * 2,
        out_specs=(pl.BlockSpec(memory_space=pltpu.VMEM),) * 2,
        scratch_shapes=[
            pltpu.VMEM((width, (tiles + 1) * rows), jnp.bfloat16),
            pltpu.VMEM((tiles * rows, rows), jnp.float32),
            pltpu.VMEM((tiles * rows, rows), jnp.bfloat16),
            pltpu.VMEM((tiles * rows, rows), jnp.bfloat16),
            pltpu.VMEM((tiles * rows, rows), jnp.bfloat16),
            pltpu.VMEM((width, plan.rounds * rows), jnp.bfloat16),
            pltpu.VMEM((width, plan.rounds * rows), jnp.bfloat16),
            pltpu.SemaphoreType.DMA((2,)),
            *[pairs_of] * 6,
        ],
        compiler_params=pltpu.CompilerParams(
            collective_id=collective_id,
            has_side_effects=True,
            vmem_limit_bytes=40 << 20,
        ),
        cost_estimate=pl.CostEstimate(
            flops=2 * (3 * tiles) * rows * rows * width,
            bytes_accessed=12 * rows * width,
            transcendentals=tiles * rows * rows,
        ),
    )(image, text)


def pick(round_bits, which):
    low = jnp.minimum(round_bits[0], round_bits[1])
    high = jnp.maximum(round_bits[0], round_bits[1])
    which[0] = high + 6 * low - ((low * (low - 1)) >> 1)


def deliver(image_from, text_from, image_out, text_out, sem):
    copies = [
        pltpu.make_async_copy(image_from, image_out, sem.at[0]),
        pltpu.make_async_copy(text_from, text_out, sem.at[1]),
    ]
    for copy in copies:
        copy.start()
    for copy in copies:
        copy.wait()


def shards(round_bits, image_embed, text_embed):
    branches = []
    for a in range(PAIR_BITS):
        for b in range(a, PAIR_BITS):
            bits = (1 << a,) if a == b else (1 << a, 1 << b)
            branches.append(functools.partial(meet, bits, len(branches) + 1))
    which = pl.pallas_call(
        pick,
        out_shape=jax.ShapeDtypeStruct((1,), jnp.int32),
        in_specs=[pl.BlockSpec(memory_space=pltpu.SMEM)],
        out_specs=pl.BlockSpec(memory_space=pltpu.SMEM),
    )(round_bits)
    grads = lax.switch(which[0], branches, image_embed.T, text_embed.T)
    image_grad, text_grad = pl.pallas_call(
        deliver,
        out_shape=tuple(jax.ShapeDtypeStruct(g.shape, g.dtype) for g in grads),
        in_specs=[pl.BlockSpec(memory_space=pl.ANY)] * 2,
        out_specs=(pl.BlockSpec(memory_space=pl.ANY),) * 2,
        scratch_shapes=[pltpu.SemaphoreType.DMA((2,))],
    )(*grads)
    return image_grad.T, text_grad.T


def solution(mesh):
    placed = (P(), P("pairs", "emb"), P("pairs", "emb"))
    return jax.shard_map(
        shards,
        mesh=mesh,
        in_specs=placed,
        out_specs=(P("pairs", "emb"), P("pairs", "emb")),
        check_vma=False,
    )
```

```python
import functools

import jax
import jax.numpy as jnp
from jax import lax
from jax.experimental import pallas as pl
from jax.experimental.pallas import tpu as pltpu
from jax.sharding import PartitionSpec as P

logit_scale = 10.0
logit_bias = -1.0
PAIR_BITS = 7
CHUNKS = 4
CHAINED = ((4, 8), (16, 64), (32, 64))
MESH = pl.DeviceIdType.MESH


def flipped(index, bit):
    return index + (1 - 2 * ((index // bit) % 2)) * bit


def last(left, right):
    return lax.dot_general(
        left, right, (((1,), (1,)), ((), ())), preferred_element_type=jnp.float32
    )


def first(left, right):
    return lax.dot_general(
        left, right, (((0,), (0,)), ((), ())), preferred_element_type=jnp.float32
    )


SCORE, WEIGH, IMAGE, ADD = range(4)


def a(tile, chunk):
    return SCORE, tile, chunk


def b(tile, chunk):
    return WEIGH, tile, chunk


def i(low, high):
    return IMAGE, low, high


def d(tile, chunk):
    return ADD, tile, chunk


ONE = [
    a(0, 0), a(0, 1), a(1, 0), a(1, 1), b(0, 0), b(0, 1), b(1, 0), a(1, 2),
    b(1, 1), a(1, 3), a(0, 2), a(0, 3), b(1, 2), b(1, 3), i(1, 1), b(0, 2),
    d(1, 0), d(1, 1), d(1, 2), b(0, 3), i(0, 0), d(1, 3),
]
TWO = [
    a(0, 0), a(0, 1), a(1, 0), a(2, 0), a(1, 1), a(2, 1), b(0, 0), b(0, 1),
    b(1, 0), b(2, 0), a(1, 2), a(2, 2), b(1, 1), b(2, 1), a(1, 3), a(2, 3),
    a(0, 2), a(0, 3), b(1, 2), b(2, 2), b(1, 3), b(2, 3), i(1, 2), b(0, 2),
    d(1, 0), d(2, 0), d(1, 1), d(2, 1), d(1, 2), d(2, 2), b(0, 3), i(0, 0),
    d(1, 3), d(2, 3),
]
CHAIN = [
    a(0, 0), a(1, 0), b(0, 0), a(1, 1), a(2, 0), a(1, 2), a(2, 1), b(2, 0),
    a(1, 3), a(2, 2), b(2, 1), a(2, 3), a(0, 1), a(0, 2), a(0, 3), b(2, 2),
    b(1, 0), b(2, 3), b(1, 1), b(1, 2), b(1, 3), i(1, 2), b(0, 1), b(0, 2),
    b(0, 3), i(0, 0), d(1, 0), d(1, 1), d(1, 2), d(1, 3),
]


class Plan:
    def __init__(self, bits):
        self.bits = bits
        self.rounds = len(bits)
        self.tiles = 1 + self.rounds
        self.chain = bits in CHAINED
        self.steps = CHAIN if self.chain else TWO if self.rounds == 2 else ONE
        images = [step for step in self.steps if step[0] == IMAGE]
        self.ahead = 2
        self.image_first = images[0][1]


def step_at(order, i):
    codes = [16 * kind + 4 * tile + chunk for kind, tile, chunk in order]
    word = 0
    for k in range(0, len(codes), 5):
        packed = sum(code << (6 * m) for m, code in enumerate(codes[k : k + 5]))
        word = jnp.where(i // 5 == k // 5, packed, word)
    code = lax.shift_right_logical(word, 6 * (i % 5)) % 64
    return code // 16, code // 4 % 4, code % 4


def kernel(
    plan,
    image_hbm,
    text_hbm,
    image_sum,
    text_sum,
    held,
    partial,
    partial_out,
    partial_in,
    weights,
    extra_out,
    extra_in,
    local_sem,
    held_send,
    held_recv,
    part_send,
    part_recv,
    extra_send,
    extra_recv,
):
    rows = image_sum.shape[1]
    n = rows // CHUNKS
    tall = image_sum.shape[0] // 2
    tiles = plan.tiles
    own = pl.ds(tiles * rows, rows)
    items = tiles * CHUNKS
    pair = lax.axis_index("pairs")
    half = lax.axis_index("emb")
    met = [flipped(pair, bit) for bit in plan.bits]
    across = flipped(met[0], plan.bits[1]) if plan.chain else None

    def place(t, c):
        return pl.ds(pl.multiple_of(t * rows + c * n, n), n)

    def back_to(t):
        if plan.rounds == 1:
            return met[0]
        return met[0] + ((across if plan.chain else met[1]) - met[0]) * (t - 1)

    def remote(src, dst, sends, recvs, t, c, device):
        return pltpu.make_async_remote_copy(
            src_ref=src,
            dst_ref=dst,
            send_sem=sends.at[t, c],
            recv_sem=recvs.at[t, c],
            device_id=device,
            device_id_type=MESH,
        )

    def held_copy(t, c, source=text_hbm, slot=0):
        return remote(
            source.at[:, place(slot, c)],
            held.at[:, place(t, c)],
            held_send,
            held_recv,
            t,
            c,
            (back_to(t), half),
        )

    def part_copy(t, c):
        return remote(
            partial_out.at[place(t, c)],
            partial_in.at[place(t, c)],
            part_send,
            part_recv,
            t,
            c,
            (pair, 1 - half),
        )

    def extra_copy(t, c):
        return remote(
            extra_out.at[:, place(t - 1, c)],
            extra_in.at[:, place(t - 1, c)],
            extra_send,
            extra_recv,
            t,
            c,
            (back_to(t), half),
        )

    own_text = pltpu.make_async_copy(text_hbm, held.at[:, pl.ds(0, rows)], local_sem.at[0])
    own_image = pltpu.make_async_copy(
        image_hbm, held.at[:, pl.ds(tiles * rows, rows)], local_sem.at[1]
    )
    own_text.start()
    own_image.start()

    peers = [(pair, 1 - half)] + [(block, half) for block in met]
    if plan.chain:
        peers.append((across, half))
    barrier = pltpu.get_barrier_semaphore()
    for peer in peers:
        pl.semaphore_signal(barrier, inc=1, device_id=peer, device_id_type=MESH)
    pl.semaphore_wait(barrier, len(peers))

    adds = plan.rounds - plan.chain

    @pl.loop(0, adds * plan.ahead)
    def _(i):
        held_copy(1 + i % adds, i // adds).start()

    own_text.wait()
    own_image.wait()

    def score(t, c):
        @pl.when(t > 0)
        def _():
            held_copy(t, c).wait_recv()

        @pl.when((t > 0) & (t <= adds) & (c + plan.ahead < CHUNKS))
        def _():
            held_copy(t, c + plan.ahead).start()

        if plan.chain:

            @pl.when(t == 1)
            def _():
                held_copy(2, c, held, 1).start()

        where = place(t, c)
        scores = first(held[:, where], held[:, own])
        partial[where, :] = scores
        partial_out[where, :] = scores.astype(jnp.bfloat16)
        part_copy(t, c).start()

    def weigh(t, c):
        part_copy(t, c).wait_recv()
        where = place(t, c)
        scores = partial[where, :] + partial_in[where, :].astype(jnp.float32)
        logits = logit_scale * scores + logit_bias
        text_row = c * n + lax.broadcasted_iota(jnp.int32, scores.shape, 0)
        image_row = lax.broadcasted_iota(jnp.int32, scores.shape, 1)
        same = text_row == image_row + t * (2 * rows)
        labels = jnp.where(same, 1.0, -1.0)
        chunk = -labels * logit_scale * jax.nn.sigmoid(-labels * logits)
        if plan.rounds == 1:
            chunk = chunk * jnp.where(t > 0, 2.0, 1.0)
        chunk = chunk.astype(jnp.bfloat16)
        weights[where, :] = chunk
        if plan.chain:

            @pl.when(t == 1)
            def _():
                extra_copy(2, c).wait_recv()

        @pl.loop(0, 2)
        def _(m):
            down = pl.ds(pl.multiple_of(m * tall, tall), tall)
            grad = last(held[down, own], weights[where, :])

            @pl.when(t == 0)
            def _():
                text_sum[down, place(0, c)] = grad

            @pl.when(t > 0)
            def _():
                extra_out[down, place(t - 1, c)] = grad.astype(jnp.bfloat16)

            if plan.chain:

                @pl.when(t == 1)
                def _():
                    extra_out[down, place(0, c)] = (
                        grad + extra_in[down, place(1, c)].astype(jnp.float32)
                    ).astype(jnp.bfloat16)

        @pl.when(t > 0)
        def _():
            extra_copy(t, c).start()

    def add_image(low, high):
        @pl.loop(low * 4, high * 4 + 4)
        def _(m):
            t = m // 4
            depth = pl.ds(pl.multiple_of(t * rows, rows), rows)
            down = pl.ds(pl.multiple_of(m // 2 % 2 * tall, tall), tall)
            block = pl.ds(pl.multiple_of(m % 2 * 256, 256), 256)
            product = jnp.dot(
                held[down, depth], weights[depth, block], preferred_element_type=jnp.float32
            )
            image_sum[down, block] = product + jnp.where(
                t == plan.image_first, 0.0, image_sum[down, block]
            )

    @pl.loop(0, len(plan.steps))
    def _(i):
        kind, t, c = step_at(plan.steps, i)

        @pl.when(kind == SCORE)
        def _():
            score(t, c)

        @pl.when(kind == WEIGH)
        def _():
            weigh(t, c)

        @pl.when(kind == IMAGE)
        def _():
            add_image(t, c)

        @pl.when(kind == ADD)
        def _():
            extra_copy(t, c).wait_recv()
            text_sum[:, place(0, c)] += extra_in[:, place(t - 1, c)].astype(jnp.float32)

    @pl.loop(0, items)
    def _(i):
        t, c = i // CHUNKS, i % CHUNKS
        part_copy(t, c).wait_send()

        @pl.when(t > 0)
        def _():
            held_copy(t, c).wait_send()
            extra_copy(t, c).wait_send()


def meet(bits, collective_id, image, text):
    plan = Plan(bits)
    width, rows = image.shape
    tiles = plan.tiles
    out = jax.ShapeDtypeStruct((width, rows), jnp.float32)
    pairs_of = pltpu.SemaphoreType.DMA((tiles, CHUNKS))
    return pl.pallas_call(
        functools.partial(kernel, plan),
        out_shape=(out, out),
        in_specs=[pl.BlockSpec(memory_space=pl.ANY)] * 2,
        out_specs=(pl.BlockSpec(memory_space=pltpu.VMEM),) * 2,
        scratch_shapes=[
            pltpu.VMEM((width, (tiles + 1) * rows), jnp.bfloat16),
            pltpu.VMEM((tiles * rows, rows), jnp.float32),
            pltpu.VMEM((tiles * rows, rows), jnp.bfloat16),
            pltpu.VMEM((tiles * rows, rows), jnp.bfloat16),
            pltpu.VMEM((tiles * rows, rows), jnp.bfloat16),
            pltpu.VMEM((width, plan.rounds * rows), jnp.bfloat16),
            pltpu.VMEM((width, plan.rounds * rows), jnp.bfloat16),
            pltpu.SemaphoreType.DMA((2,)),
            *[pairs_of] * 6,
        ],
        compiler_params=pltpu.CompilerParams(
            collective_id=collective_id,
            has_side_effects=True,
            vmem_limit_bytes=40 << 20,
        ),
        cost_estimate=pl.CostEstimate(
            flops=2 * (3 * tiles) * rows * rows * width,
            bytes_accessed=12 * rows * width,
            transcendentals=tiles * rows * rows,
        ),
    )(image, text)


def pick(round_bits, which):
    low = jnp.minimum(round_bits[0], round_bits[1])
    high = jnp.maximum(round_bits[0], round_bits[1])
    which[0] = high + 6 * low - ((low * (low - 1)) >> 1)


def deliver(image_from, text_from, image_out, text_out, sem):
    copies = [
        pltpu.make_async_copy(image_from, image_out, sem.at[0]),
        pltpu.make_async_copy(text_from, text_out, sem.at[1]),
    ]
    for copy in copies:
        copy.start()
    for copy in copies:
        copy.wait()


def shards(round_bits, image_embed, text_embed):
    branches = []
    for a in range(PAIR_BITS):
        for b in range(a, PAIR_BITS):
            bits = (1 << a,) if a == b else (1 << a, 1 << b)
            branches.append(functools.partial(meet, bits, len(branches) + 1))
    which = pl.pallas_call(
        pick,
        out_shape=jax.ShapeDtypeStruct((1,), jnp.int32),
        in_specs=[pl.BlockSpec(memory_space=pltpu.SMEM)],
        out_specs=pl.BlockSpec(memory_space=pltpu.SMEM),
    )(round_bits)
    grads = lax.switch(which[0], branches, image_embed.T, text_embed.T)
    image_grad, text_grad = pl.pallas_call(
        deliver,
        out_shape=tuple(jax.ShapeDtypeStruct(g.shape, g.dtype) for g in grads),
        in_specs=[pl.BlockSpec(memory_space=pl.ANY)] * 2,
        out_specs=(pl.BlockSpec(memory_space=pl.ANY),) * 2,
        scratch_shapes=[pltpu.SemaphoreType.DMA((2,))],
    )(*grads)
    return image_grad.T, text_grad.T


def solution(mesh):
    placed = (P(), P("pairs", "emb"), P("pairs", "emb"))
    return jax.shard_map(
        shards,
        mesh=mesh,
        in_specs=placed,
        out_specs=(P("pairs", "emb"), P("pairs", "emb")),
        check_vma=False,
    )
```
